32 devices in a mesh: wide: 8 (over z, x), narrow: 4 (over y, core).
Axes of the slice: x: 2, y: 2, z: 4, core: 2. Of those that a mesh axis runs over, the one named last changes fastest.
Arguments:
- design: float32 [65536, 128], P(('wide', 'narrow')), may hold values from 0.05 to 1
- filter_tiles: float32 [5, 128, 128], replicated
- filter_cols: int32 [65536, 5], P(('wide', 'narrow')), may hold values from -1 to 65535, as said below
- slot_block: int32 [65536], P(('wide', 'narrow')), may hold values from 0 to 65535, as said below
- holes: int32 [1024, 8192], P('wide', 'narrow'), may hold values 0 or 1
- squeeze_source: float32 [1024, 8192], P('wide', 'narrow'), may hold values from -6 to 6
- force_weight: float32 [1024, 8192], P('wide', 'narrow'), may hold values from 0.2 to 2
Outputs:
- pressure: float32 [1024, 8192], P('wide', 'narrow')
- sensitivity: float32 [65536, 128], P(('wide', 'narrow'))
The draws below stay inside these ranges and needn't reach their ends.
Inputs may be any that keep to these rules, and one draw needn't show every extreme that they name: `slot_block`: film blocks are ordered along a curve that visits the tiles in order and, inside a tile of 16 x 128 blocks, the blocks in Morton order (column bit lowest); for one stagger h with 512 <= h <= 1536, design slot s controls the block at curve position (s + h) mod 65536. So the slots of owner d (slots d * 2048 to (d + 1) * 2048 - 1) lie in tiles d and d + 1, those of the last owner in its own tile and tile 0. filter_cols[r, 0] = r; entries 1 to 4 are the design slots of the film blocks above, below, left and right of the block of slot r inside the same tile, -1 where that neighbour lies outside the tile.
All inputs are finite; a program needn't handle non-finite values. No bound on the sum of `holes` on one device may be relied on, other than what follows from the above.
Results may differ from the reference program's by a relative error of at most 0.00025.
Values sent between devices are 32-bit elements; how exact they have to be, the bound alone decides.
A program may use at most 192 MiB of HBM per device.

```python
import math
import jax
import jax.numpy as jnp
from jax import lax

CR = 128
CC = 2048
SWEEPS = 16
KNB = 5
BLOCK = 128
SLOTS = 2048
NB = 65536
NR = 1024
NC = 8192
N_WIDE = 8
N_NARROW = 4


def draw_filter_tiles(key, part):
    logs = jax.random.uniform(jax.random.fold_in(key, 11), (KNB, 128, 128), jnp.float32, jnp.log(0.02), jnp.log(0.5))
    tiles = jnp.exp(logs) * (2.0 / 128.0)
    identity = jnp.eye(128, dtype=jnp.float32)
    return tiles.at[0].add(identity)


def stagger_of(key):
    return jax.random.randint(jax.random.fold_in(key, 41), (), SLOTS // 4, 3 * SLOTS // 4 + 1).astype(jnp.int32)


def bit_widths():
    return ((CR // 8).bit_length() - 1, (CC // 16).bit_length() - 1)


def decode_inner(inner):
    row_bits, col_bits = bit_widths()
    shared = min(row_bits, col_bits)
    block_row = jnp.zeros_like(inner)
    block_col = jnp.zeros_like(inner)
    place = 0
    for level in range(shared):
        block_col = block_col + inner // 2 ** place % 2 * 2 ** level
        place = place + 1
        block_row = block_row + inner // 2 ** place % 2 * 2 ** level
        place = place + 1
    for level in range(shared, row_bits):
        block_row = block_row + inner // 2 ** place % 2 * 2 ** level
        place = place + 1
    for level in range(shared, col_bits):
        block_col = block_col + inner // 2 ** place % 2 * 2 ** level
        place = place + 1
    return (block_row, block_col)


def encode_inner(block_row, block_col):
    row_bits, col_bits = bit_widths()
    shared = min(row_bits, col_bits)
    inner = jnp.zeros_like(block_row)
    place = 0
    for level in range(shared):
        inner = inner + block_col // 2 ** level % 2 * 2 ** place
        place = place + 1
        inner = inner + block_row // 2 ** level % 2 * 2 ** place
        place = place + 1
    for level in range(shared, row_bits):
        inner = inner + block_row // 2 ** level % 2 * 2 ** place
        place = place + 1
    for level in range(shared, col_bits):
        inner = inner + block_col // 2 ** level % 2 * 2 ** place
        place = place + 1
    return inner


def draw_slot_block(key, part):
    slots_all = jnp.arange(NB, dtype=jnp.int32)
    position = (slots_all + stagger_of(key)) % NB
    tile = position // SLOTS
    block_row, block_col = decode_inner(position % SLOTS)
    return (tile * SLOTS + block_row * (CC // 16) + block_col).astype(jnp.int32)


def draw_filter_cols(key, part):
    shift = stagger_of(key)
    slots_all = jnp.arange(NB, dtype=jnp.int32)
    position = (slots_all + shift) % NB
    tile = position // SLOTS
    block_row, block_col = decode_inner(position % SLOTS)
    columns = [slots_all]
    for row_step, col_step in ((-1, 0), (1, 0), (0, -1), (0, 1)):
        near_row = block_row + row_step
        near_col = block_col + col_step
        inside = (near_row >= 0) & (near_row < CR // 8) & (near_col >= 0) & (near_col < CC // 16)
        safe_row = jnp.clip(near_row, 0, CR // 8 - 1)
        safe_col = jnp.clip(near_col, 0, CC // 16 - 1)
        near_position = tile * SLOTS + encode_inner(safe_row, safe_col)
        near_slot = (near_position - shift + NB) % NB
        columns.append(jnp.where(inside, near_slot, -1))
    return jnp.stack(columns, axis=1).astype(jnp.int32)


def place_ends(values, rng, smallest, high):
    longest = values.shape.index(max(values.shape))
    spots = []
    for shift in (0, 1):
        where = [jax.random.randint(jax.random.fold_in(rng, axis), (), 0, length) for axis, length in enumerate(values.shape)]
        where[longest] = (where[longest] + shift) % values.shape[longest]
        spots.append(tuple(where))
    return values.at[spots[0]].set(smallest).at[spots[1]].set(high)


def shard_levels(own_key, dims, shards, low, top_value):
    def one(axis_at, parts):
        steps = jax.random.uniform(jax.random.fold_in(jax.random.fold_in(own_key, 6), axis_at), (parts,), jnp.float32, low / len(shards), top_value / len(shards))
        return jnp.repeat(jnp.exp(steps), dims[axis_at] // parts).reshape((-1,) + (1,) * (len(dims) - axis_at - 1))

    factor_of = one(*shards[0])
    for cut in shards[1:]:
        factor_of = factor_of * one(*cut)
    return factor_of


def bell_draw(own_key, extent, width, bound, shards=(), held_as=jnp.bfloat16):
    loudness = shard_levels(own_key, extent, shards, -0.22, 0.18) if shards else 1.0
    values = jax.random.normal(own_key, extent, jnp.float32) * width * loudness
    return jnp.minimum(jnp.maximum(values, -bound), bound).astype(held_as)


def setup_inputs(seed: int = 0) -> dict:
    keys = jax.random.split(jax.random.key(seed), 8)
    design = jnp.clip(0.05 + 0.95 * jax.random.uniform(keys[0], (NB, BLOCK), jnp.float32) ** shard_levels(keys[0], (NB, BLOCK), ((0, 32),), -0.2, 0.2), 0.05, 1.0)
    filter_tiles = draw_filter_tiles(jax.random.fold_in(keys[7], 71), 0)
    filter_cols = draw_filter_cols(jax.random.fold_in(keys[7], 71), 0)
    slot_block = draw_slot_block(jax.random.fold_in(keys[7], 71), 0)
    holes = place_ends((jax.random.randint(keys[4], (NR, NC), 0, 8) < 1).astype(jnp.int32), jax.random.fold_in(keys[4], 1), 0, 1)
    squeeze_source = bell_draw(keys[5], (NR, NC), 1.0, 6.0, ((0, 8), (1, 4)), jnp.float32)
    force_weight = jnp.clip(jnp.exp(math.log(2.0) - 2.3025851 * jax.random.uniform(keys[6], (NR, NC), jnp.float32) ** shard_levels(keys[6], (NR, NC), ((0, 8), (1, 4)), -0.2, 0.2)), 0.2, 2.0)
    return {"design": design, "filter_tiles": filter_tiles, "filter_cols": filter_cols, "slot_block": slot_block, "holes": holes, "squeeze_source": squeeze_source, "force_weight": force_weight}


COND_FLOOR = 0.01
SQUEEZE_DAMPING = 0.25
FULL_PRECISION = lax.Precision.HIGHEST


def relax(fields, conduct, sources, solid_mask, rim_depth, outer_rim):
    offset = outer_rim - rim_depth + 1
    inner_rows = fields.shape[1] - 2
    inner_cols = fields.shape[2] - 2

    def window(values, row_step, col_step):
        return values[..., offset + row_step:offset + row_step + inner_rows, offset + col_step:offset + col_step + inner_cols]

    k_here = window(conduct, 0, 0)
    face_north = 0.5 * (k_here + window(conduct, -1, 0))
    face_south = 0.5 * (k_here + window(conduct, 1, 0))
    face_west = 0.5 * (k_here + window(conduct, 0, -1))
    face_east = 0.5 * (k_here + window(conduct, 0, 1))
    coupled = face_north * fields[:, 0:inner_rows, 1:inner_cols + 1]
    coupled = coupled + face_south * fields[:, 2:inner_rows + 2, 1:inner_cols + 1]
    coupled = coupled + face_west * fields[:, 1:inner_rows + 1, 0:inner_cols]
    coupled = coupled + face_east * fields[:, 1:inner_rows + 1, 2:inner_cols + 2]
    diagonal = face_north + face_south + face_west + face_east + SQUEEZE_DAMPING
    return (window(sources, 0, 0) + coupled) / diagonal * window(solid_mask, 0, 0)


def film_gradient(padded, density):
    row_count = padded.shape[1] - 2
    col_count = padded.shape[2] - 2
    p_here = padded[0, 1:row_count + 1, 1:col_count + 1]
    a_here = padded[1, 1:row_count + 1, 1:col_count + 1]
    summed = jnp.zeros((row_count, col_count), jnp.float32)
    for row_start, col_start in ((0, 1), (2, 1), (1, 0), (1, 2)):
        nearby = padded[:, row_start:row_start + row_count, col_start:col_start + col_count]
        summed = summed + (a_here - nearby[1]) * (p_here - nearby[0])
    return -0.5 * summed * (3.0 * (1.0 - COND_FLOOR)) * density * density


def reference(design, filter_tiles, filter_cols, slot_block, holes, squeeze_source, force_weight):
    present = filter_cols >= 0
    safe_cols = jnp.where(present, filter_cols, 0).astype(jnp.int32)
    picked = jnp.where(present[:, :, None], design[safe_cols], 0.0)
    numer = jnp.einsum('rkj,kij->ri', picked, filter_tiles, precision=FULL_PRECISION)
    denom = jnp.dot(present.astype(jnp.float32), jnp.sum(filter_tiles, axis=2), precision=FULL_PRECISION)
    filtered = numer / denom
    placed = jnp.zeros((NB, 128), jnp.float32).at[slot_block].set(filtered)
    density = placed.reshape(N_WIDE, N_NARROW, CR // 8, CC // 16, 8, 16).transpose(0, 2, 4, 1, 3, 5).reshape(NR, NC)
    conduct = COND_FLOOR + (1.0 - COND_FLOOR) * density * density * density
    solid_mask = jnp.where(holes > 0, 0.0, 1.0).astype(jnp.float32)
    sources = jnp.stack([squeeze_source, force_weight])
    conduct_pad = jnp.pad(conduct, 1)
    sources_pad = jnp.pad(sources, ((0, 0), (1, 1), (1, 1)))
    solid_pad = jnp.pad(solid_mask, 1)
    fields = jnp.zeros((2, NR, NC), jnp.float32)
    for sweep_index in range(SWEEPS):
        fields = relax(jnp.pad(fields, ((0, 0), (1, 1), (1, 1))), conduct_pad, sources_pad, solid_pad, 1, 1)
    film_sens = film_gradient(jnp.pad(fields, ((0, 0), (1, 1), (1, 1))), density)
    film_blocks = film_sens.reshape(N_WIDE, CR // 8, 8, N_NARROW, CC // 16, 16).transpose(0, 3, 1, 4, 2, 5).reshape(NB, 128)
    returned = film_blocks[slot_block]
    scaled = returned / denom
    spread = jnp.einsum('ri,kij->rkj', scaled, filter_tiles, precision=FULL_PRECISION)
    spread = jnp.where(present[:, :, None], spread, 0.0)
    sensitivity = jnp.zeros((NB, 128), jnp.float32).at[safe_cols].add(spread)
    return fields[0], sensitivity
```

```python
import functools

import jax
import jax.numpy as jnp
from jax import lax
from jax.experimental import pallas as pl
from jax.experimental.pallas import tpu as pltpu
from jax.sharding import PartitionSpec as P

SWEEPS = 16
COND_FLOOR = 0.01
SQUEEZE_DAMPING = 0.25
MESH = pl.DeviceIdType.MESH

SLOTS = 2048
RIM = 24
ROWS = 128
TALL = ROWS + 2 * RIM
STRIPS = 16
WIDE = STRIPS + 1
SENT = 1536
GROUP = 256
GROUPS = SLOTS // GROUP
SENT_GROUPS = SENT // GROUP

DESIGN, ST_L, ST_R, ST_U, ST_D, K_L, K_R, K_U, K_D, BACK = range(10)
COPIES = BACK + SENT_GROUPS


def sub_bit(bit):
    return (lax.broadcasted_iota(jnp.int32, (8, 128), 0) // bit) % 2


def swap_middle(x):
    b1, b2 = sub_bit(2), sub_bit(4)
    moved = jnp.where(b1 == 1, pltpu.roll(x, 6, 0), pltpu.roll(x, 2, 0))
    return jnp.where(b1 == b2, x, moved)


def curve_to_rows(group):
    low = sub_bit(2) == 0
    out = {}
    for r3 in range(2):
        for c3 in range(2):
            for r2 in range(2):
                for r1 in range(2):
                    at = 8 * (r1 + 4 * r2 + 8 * c3 + 16 * r3)
                    a, b = group[at : at + 8], group[at + 16 : at + 24]
                    row = 2 * r1 + 4 * r2 + 8 * r3
                    even = jnp.where(low, a, pltpu.roll(b, 2, 0))
                    odd = jnp.where(low, pltpu.roll(a, 6, 0), b)
                    out[row, c3] = swap_middle(even)
                    out[row + 1, c3] = swap_middle(odd)
    return out


def rows_to_curve(group):
    low = sub_bit(2) == 0
    out = [None] * 32
    for r3 in range(2):
        for c3 in range(2):
            for r2 in range(2):
                for r1 in range(2):
                    row = 2 * r1 + 4 * r2 + 8 * r3
                    at = row * 16 + 8 * c3
                    even = swap_middle(group[at : at + 8])
                    odd = swap_middle(group[at + 16 : at + 24])
                    v = r1 + 4 * r2 + 8 * c3 + 16 * r3
                    out[v] = jnp.where(low, even, pltpu.roll(odd, 2, 0))
                    out[v + 2] = jnp.where(low, pltpu.roll(even, 6, 0), odd)
    return out


def flip_block(x):
    chunk = lax.broadcasted_iota(jnp.int32, (8, 128), 1) // 16
    for bit in (1, 2):
        s, c = sub_bit(bit), (chunk // bit) % 2
        up = pltpu.roll(pltpu.roll(x, 8 - bit, 0), 16 * bit, 1)
        down = pltpu.roll(pltpu.roll(x, bit, 0), 128 - 16 * bit, 1)
        x = jnp.where(s == c, x, jnp.where(c == 1, up, down))
    both = pltpu.roll(pltpu.roll(x, 4, 0), 64, 1)
    return jnp.where(sub_bit(4) == chunk // 4, x, both)


def split(x):
    hi = x.astype(jnp.bfloat16)
    lo = (x - hi.astype(jnp.float32)).astype(jnp.bfloat16)
    return hi, lo


def product(lhs, weights):
    hi, lo = split(lhs)
    full = jnp.dot(hi, weights, preferred_element_type=jnp.float32)
    rest = jnp.dot(lo, weights, preferred_element_type=jnp.float32)
    return full[:, :128] + (full[:, 128:] + (rest[:, :128] + rest[:, 128:]))


def body(
    n_wide, n_narrow,
    slot_ref, design_ref, tiles_ref, holes_ref, squeeze_ref, force_ref,
    pressure_ref, sens_ref,
    ext, blocks, curve, wf, wb, sums, st, st_l, st_r, k_l, k_r,
    cond, dens, wn, ws, ww, we, src, fields, send, recv,
):
    w, n = lax.axis_index("wide"), lax.axis_index("narrow")
    owners = n_wide * n_narrow
    me = w * n_narrow + n
    after = lax.rem(me + 1, owners)
    before = lax.rem(me + owners - 1, owners)
    nxt = (after // n_narrow, lax.rem(after, n_narrow))
    prv = (before // n_narrow, lax.rem(before, n_narrow))
    up = (lax.rem(w + n_wide - 1, n_wide), n)
    down = (lax.rem(w + 1, n_wide), n)
    left = (w, lax.rem(n + n_narrow - 1, n_narrow))
    right = (w, lax.rem(n + 1, n_narrow))
    has_up, has_down = w > 0, w < n_wide - 1
    has_left, has_right = n > 0, n < n_narrow - 1

    barrier = pltpu.get_barrier_semaphore()
    pl.semaphore_signal(barrier, inc=1, device_id=nxt, device_id_type=MESH)
    pl.semaphore_signal(barrier, inc=1, device_id=prv, device_id_type=MESH)
    for there, device in ((has_up, up), (has_down, down), (has_left, left), (has_right, right)):
        @pl.when(there)
        def _():
            pl.semaphore_signal(barrier, inc=1, device_id=device, device_id_type=MESH)
    expected = 2 + sum(jnp.where(t, 1, 0) for t in (has_up, has_down, has_left, has_right))
    pl.semaphore_wait(barrier, expected)

    def remote(which, src_ref, dst_ref, device):
        return pltpu.make_async_remote_copy(
            src_ref=src_ref, dst_ref=dst_ref,
            send_sem=send.at[which], recv_sem=recv.at[which],
            device_id=device, device_id_type=MESH,
        )

    tile_rows = pl.ds(RIM, ROWS)
    top_rows, low_rows = pl.ds(RIM, RIM), pl.ds(ROWS, RIM)
    above_rows, below_rows = pl.ds(0, RIM), pl.ds(RIM + ROWS, RIM)
    design_copy = remote(DESIGN, design_ref.at[pl.ds(SLOTS - SENT, SENT)], ext.at[pl.ds(0, SENT)], nxt)
    st_left = remote(ST_L, st.at[:, 0, tile_rows], st_r, left)
    st_right = remote(ST_R, st.at[:, STRIPS - 1, tile_rows], st_l, right)
    st_up = remote(ST_U, st.at[:, :, top_rows], st.at[:, :, below_rows], up)
    st_down = remote(ST_D, st.at[:, :, low_rows], st.at[:, :, above_rows], down)
    k_left = remote(K_L, cond.at[0, tile_rows], k_r, left)
    k_right = remote(K_R, cond.at[STRIPS - 1, tile_rows], k_l, right)
    k_up = remote(K_U, cond.at[:, top_rows], cond.at[:, below_rows], up)
    k_down = remote(K_D, cond.at[:, low_rows], cond.at[:, above_rows], down)

    def start_pair(first, has_first, second, has_second):
        pl.when(has_first)(first.start)
        pl.when(has_second)(second.start)

    def wait_pair(first, has_first, second, has_second):
        pl.when(has_first)(first.wait_send)
        pl.when(has_second)(second.wait_send)
        pl.when(has_second)(first.wait_recv)
        pl.when(has_first)(second.wait_recv)

    design_copy.start()

    for g in range(STRIPS):
        cols = pl.ds(g * 128, 128)
        st[0, g, tile_rows, :] = squeeze_ref[:, cols]
        st[1, g, tile_rows, :] = force_ref[:, cols]
        st[2, g, tile_rows, :] = jnp.where(holes_ref[:, cols] > 0, 0.0, 1.0).astype(jnp.float32)
    start_pair(st_left, has_left, st_right, has_right)

    ext[pl.ds(SENT, SLOTS), :] = design_ref[...]
    blocks[...] = jnp.zeros(blocks.shape, jnp.float32)
    for k in range(5):
        tile = tiles_ref[k]
        turned = tile.T
        rows = pl.ds(k * 128, 128)
        hi, lo = split(turned)
        wf[rows, pl.ds(0, 128)] = hi
        wf[rows, pl.ds(128, 128)] = lo
        hi, lo = split(tile)
        wb[rows, pl.ds(0, 128)] = hi
        wb[rows, pl.ds(128, 128)] = lo
        sums[pl.ds(k, 1), :] = jnp.sum(turned, axis=0, keepdims=True)

    for there, value in ((has_left, st_l), (has_right, st_r)):
        @pl.when(jnp.logical_not(there))
        def _():
            value[...] = jnp.zeros(value.shape, jnp.float32)
    for there, value in ((has_left, k_l), (has_right, k_r)):
        @pl.when(jnp.logical_not(there))
        def _():
            value[...] = jnp.zeros(value.shape, jnp.float32)
    for there, rows in ((has_up, above_rows), (has_down, below_rows)):
        @pl.when(jnp.logical_not(there))
        def _():
            st[:, :, rows, :] = jnp.zeros((3, WIDE, RIM, 128), jnp.float32)
            cond[:, rows, :] = jnp.zeros((WIDE, RIM, 128), jnp.float32)

    wait_pair(st_left, has_left, st_right, has_right)
    lane = lax.broadcasted_iota(jnp.int32, (ROWS, 128), 1)
    for q in range(3):
        st[q, STRIPS, tile_rows, :] = jnp.where(lane < 64, st_r[q], st_l[q])
    start_pair(st_up, has_up, st_down, has_down)

    first = slot_ref[0]
    block_row, block_col = (first // 128) % 16, first % 128
    stagger = (block_col // 16) * 256
    for level in range(4):
        stagger = stagger + (block_col // 2**level) % 2 * 4**level
        stagger = stagger + (block_row // 2**level) % 2 * (2 * 4**level)

    design_copy.wait()
    offset = SENT - stagger

    def place(c, _):
        group = ext[pl.ds(offset + c * GROUP, GROUP), :]
        for (row, half), value in curve_to_rows(group).items():
            at = pl.multiple_of(8 + 16 * c + 8 * half, 8)
            blocks[1 + row, pl.ds(at, 8), :] = value
        return 0

    lax.fori_loop(0, GROUPS, place, 0)

    def near(c):
        def take(row, col):
            return blocks[pl.ds(1 + row, 16), pl.ds(8 + 16 * c + col, 16), :].reshape(GROUP, 128)
        return take

    def denominator(c, width, count):
        row = lax.broadcasted_iota(jnp.int32, (16, width, 128), 0)
        col = lax.broadcasted_iota(jnp.int32, (16, width, 128), 1) + c * width
        total = jnp.broadcast_to(sums[pl.ds(0, 1), :].reshape(1, 1, 128), row.shape)
        inside = (row > 0, row < 15, col > 0, col < 127)
        for k in range(4):
            total = total + jnp.where(inside[k], sums[pl.ds(k + 1, 1), :].reshape(1, 1, 128), 0.0)
        return total.reshape(count, 128)

    def forward(c, _):
        take = near(c)
        lhs = jnp.concatenate([take(0, 0), take(-1, 0), take(1, 0), take(0, -1), take(0, 1)], axis=1)
        filtered = product(lhs, wf[...]) / denominator(c, 16, GROUP)
        for row in range(16):
            for half in range(2):
                at = row * 16 + 8 * half
                film = flip_block(filtered[at : at + 8])
                dens[2 * c + half, pl.ds(row * 8, 8), :] = film
                cond[2 * c + half, pl.ds(RIM + row * 8, 8), :] = (
                    COND_FLOOR + (1.0 - COND_FLOOR) * film * film * film
                )
        return 0

    lax.fori_loop(0, GROUPS, forward, 0)
    start_pair(k_left, has_left, k_right, has_right)
    wait_pair(k_left, has_left, k_right, has_right)
    cond[STRIPS, tile_rows, :] = jnp.where(lane < 64, k_r[...], k_l[...])
    start_pair(k_up, has_up, k_down, has_down)

    lane8 = lax.broadcasted_iota(jnp.int32, (8, 128), 1)

    def sides(row):
        out = []
        for g in range(WIDE):
            west = pltpu.roll(jnp.where(lane8 == 127, row[g - 1], row[g]), 1, 1)
            east = pltpu.roll(jnp.where(lane8 == 0, row[(g + 1) % WIDE], row[g]), 127, 1)
            out.append((west, east))
        return out

    def coefficients(step, _):
        r = pl.multiple_of(step * 8, 8)
        here = [cond[g, pl.ds(r, 8), :] for g in range(WIDE)]
        beside = sides(here)
        for g in range(WIDE):
            k = here[g]
            north = 0.5 * (k + cond[g, pl.ds(r - 1, 8), :])
            south = 0.5 * (k + cond[g, pl.ds(r + 1, 8), :])
            west = 0.5 * (k + beside[g][0])
            east = 0.5 * (k + beside[g][1])
            inverse = 1.0 / (north + south + west + east + SQUEEZE_DAMPING)
            solid = st[2, g, pl.ds(r, 8), :] > 0.5
            for ref, face in ((wn, north), (ws, south), (ww, west), (we, east)):
                ref[g, pl.ds(r, 8), :] = jnp.where(solid, face * inverse, 0.0)
            for q in range(2):
                value = jnp.where(solid, st[q, g, pl.ds(r, 8), :] * inverse, 0.0)
                src[q, g, pl.ds(r, 8), :] = value
                fields[0, q, g, pl.ds(r, 8), :] = value
        return 0

    lax.fori_loop(4, 18, coefficients, 0)
    wait_pair(st_up, has_up, st_down, has_down)
    wait_pair(k_up, has_up, k_down, has_down)
    lax.fori_loop(1, 4, coefficients, 0)
    lax.fori_loop(18, 21, coefficients, 0)

    def sweep(first_step, last_step):
        def run(index, _):
            old, new = index % 2, (index + 1) % 2

            def one(step, _):
                r = pl.multiple_of(step * 8, 8)
                rows = pl.ds(r, 8)
                here = [[fields[old, q, g, rows, :] for g in range(WIDE)] for q in range(2)]
                beside = [sides(here[q]) for q in range(2)]
                for g in range(WIDE):
                    a, b, c, d = wn[g, rows, :], ws[g, rows, :], ww[g, rows, :], we[g, rows, :]
                    for q in range(2):
                        north = fields[old, q, g, pl.ds(r - 1, 8), :]
                        south = fields[old, q, g, pl.ds(r + 1, 8), :]
                        west, east = beside[q][g]
                        fields[new, q, g, rows, :] = (src[q, g, rows, :] + a * north + b * south) + (
                            c * west + d * east
                        )
                return 0

            lax.fori_loop(first_step, last_step, one, 0)
            return 0

        return run

    lax.fori_loop(0, 7, sweep(1, 21), 0)
    lax.fori_loop(7, SWEEPS - 1, sweep(2, 20), 0)
    last = (SWEEPS - 1) % 2

    def gradient(g, _):
        summed = jnp.zeros((ROWS, 128), jnp.float32)
        p = fields[last, 0, g, tile_rows, :]
        a = fields[last, 1, g, tile_rows, :]
        pressure_ref[:, pl.ds(pl.multiple_of(g * 128, 128), 128)] = p
        for shift in (RIM - 1, RIM + 1):
            rows = pl.ds(shift, ROWS)
            summed = summed + (a - fields[last, 1, g, rows, :]) * (p - fields[last, 0, g, rows, :])
        west, east = lax.rem(g + STRIPS, WIDE), g + 1
        for edge, strip, turn in ((127, west, 1), (0, east, 127)):
            pn = pltpu.roll(jnp.where(lane == edge, fields[last, 0, strip, tile_rows, :], p), turn, 1)
            an = pltpu.roll(jnp.where(lane == edge, fields[last, 1, strip, tile_rows, :], a), turn, 1)
            summed = summed + (a - an) * (p - pn)
        density = dens[g]
        sens = -0.5 * summed * (3.0 * (1.0 - COND_FLOOR)) * density * density
        scale = denominator(g, 8, ROWS)
        at = pl.multiple_of(8 + 8 * g, 8)
        for row in range(16):
            part = slice(row * 8, row * 8 + 8)
            blocks[1 + row, pl.ds(at, 8), :] = flip_block(sens[part]) / scale[part]
        return 0

    lax.fori_loop(0, STRIPS, gradient, 0)

    def back_copy(c):
        return remote(BACK + c, curve.at[pl.ds(c * GROUP, GROUP)], curve.at[pl.ds(SLOTS + c * GROUP, GROUP)], prv)

    def backward(c):
        take = near(c)
        lhs = jnp.concatenate([take(0, 0), take(1, 0), take(-1, 0), take(0, 1), take(0, -1)], axis=1)
        for v, value in enumerate(rows_to_curve(product(lhs, wb[...]))):
            at = c * GROUP + 8 * v
            if not isinstance(at, int):
                at = pl.multiple_of(at, 8)
            curve[pl.ds(at, 8), :] = value

    for c in range(GROUPS):
        backward(c)
        if c < SENT_GROUPS:
            back_copy(c).start()
    for c in range(SENT_GROUPS):
        back_copy(c).wait()

    def give(c, _):
        at = pl.multiple_of(c * GROUP, GROUP)
        sens_ref[pl.ds(at, GROUP), :] = curve[pl.ds(stagger + c * GROUP, GROUP), :]
        return 0

    lax.fori_loop(0, GROUPS, give, 0)


def solution(mesh):
    n_wide, n_narrow = mesh.shape["wide"], mesh.shape["narrow"]
    f32, bf16 = jnp.float32, jnp.bfloat16
    vmem = pl.BlockSpec(memory_space=pltpu.VMEM)

    def local(design, filter_tiles, filter_cols, slot_block, holes, squeeze_source, force_weight):
        strips = (WIDE, TALL, 128)
        return pl.pallas_call(
            functools.partial(body, n_wide, n_narrow),
            out_shape=(
                jax.ShapeDtypeStruct(holes.shape, f32),
                jax.ShapeDtypeStruct(design.shape, f32),
            ),
            in_specs=[pl.BlockSpec(memory_space=pltpu.SMEM)] + [vmem] * 5,
            out_specs=(vmem, vmem),
            scratch_shapes=[
                pltpu.VMEM((SENT + SLOTS + 8, 128), f32),
                pltpu.VMEM((18, 144, 128), f32),
                pltpu.VMEM((SENT + SLOTS + 8, 128), f32),
                pltpu.VMEM((640, 256), bf16),
                pltpu.VMEM((640, 256), bf16),
                pltpu.VMEM((8, 128), f32),
                pltpu.VMEM((3,) + strips, f32),
                pltpu.VMEM((3, ROWS, 128), f32),
                pltpu.VMEM((3, ROWS, 128), f32),
                pltpu.VMEM((ROWS, 128), f32),
                pltpu.VMEM((ROWS, 128), f32),
                pltpu.VMEM(strips, f32),
                pltpu.VMEM((STRIPS, ROWS, 128), f32),
                pltpu.VMEM(strips, f32),
                pltpu.VMEM(strips, f32),
                pltpu.VMEM(strips, f32),
                pltpu.VMEM(strips, f32),
                pltpu.VMEM((2,) + strips, f32),
                pltpu.VMEM((2, 2) + strips, f32),
                pltpu.SemaphoreType.DMA((COPIES,)),
                pltpu.SemaphoreType.DMA((COPIES,)),
            ],
            compiler_params=pltpu.CompilerParams(
                collective_id=0, has_side_effects=True, vmem_limit_bytes=56 * 2**20
            ),
        )(slot_block, design, filter_tiles, holes, squeeze_source, force_weight)

    placed = (
        P(("wide", "narrow"), None),
        P(),
        P(("wide", "narrow"), None),
        P(("wide", "narrow")),
        P("wide", "narrow"),
        P("wide", "narrow"),
        P("wide", "narrow"),
    )
    return jax.shard_map(
        local,
        mesh=mesh,
        in_specs=placed,
        out_specs=(P("wide", "narrow"), P(("wide", "narrow"), None)),
        check_vma=False,
    )
```

```python
import functools

import jax
import jax.numpy as jnp
from jax import lax
from jax.experimental import pallas as pl
from jax.experimental.pallas import tpu as pltpu
from jax.sharding import PartitionSpec as P

SWEEPS = 16
COND_FLOOR = 0.01
SQUEEZE_DAMPING = 0.25
MESH = pl.DeviceIdType.MESH

SLOTS = 2048
RIM = 24
ROWS = 128
TALL = ROWS + 2 * RIM
STRIPS = 16
WIDE = STRIPS + 1
SENT = 1536
GROUP = 256
GROUPS = SLOTS // GROUP
SENT_GROUPS = SENT // GROUP

DEEP = 16
DESIGN, ST_L, ST_R, ST_U, ST_D, K_L, K_R = range(7)
K_U = 7
K_D = K_U + GROUPS + 1
BACK = K_D + GROUPS + 1
COPIES = BACK + SENT_GROUPS


def sub_bit(bit):
    return (lax.broadcasted_iota(jnp.int32, (8, 128), 0) // bit) % 2


def swap_middle(x):
    b1, b2 = sub_bit(2), sub_bit(4)
    moved = jnp.where(b1 == 1, pltpu.roll(x, 6, 0), pltpu.roll(x, 2, 0))
    return jnp.where(b1 == b2, x, moved)


def curve_to_rows(group):
    low = sub_bit(2) == 0
    out = {}
    for r3 in range(2):
        for c3 in range(2):
            for r2 in range(2):
                for r1 in range(2):
                    at = 8 * (r1 + 4 * r2 + 8 * c3 + 16 * r3)
                    a, b = group[at : at + 8], group[at + 16 : at + 24]
                    row = 2 * r1 + 4 * r2 + 8 * r3
                    even = jnp.where(low, a, pltpu.roll(b, 2, 0))
                    odd = jnp.where(low, pltpu.roll(a, 6, 0), b)
                    out[row, c3] = swap_middle(even)
                    out[row + 1, c3] = swap_middle(odd)
    return out


def rows_to_curve(group):
    low = sub_bit(2) == 0
    out = [None] * 32
    for r3 in range(2):
        for c3 in range(2):
            for r2 in range(2):
                for r1 in range(2):
                    row = 2 * r1 + 4 * r2 + 8 * r3
                    at = row * 16 + 8 * c3
                    even = swap_middle(group[at : at + 8])
                    odd = swap_middle(group[at + 16 : at + 24])
                    v = r1 + 4 * r2 + 8 * c3 + 16 * r3
                    out[v] = jnp.where(low, even, pltpu.roll(odd, 2, 0))
                    out[v + 2] = jnp.where(low, pltpu.roll(even, 6, 0), odd)
    return out


def flip_block(x):
    chunk = lax.broadcasted_iota(jnp.int32, (8, 128), 1) // 16
    for bit in (1, 2):
        s, c = sub_bit(bit), (chunk // bit) % 2
        up = pltpu.roll(pltpu.roll(x, 8 - bit, 0), 16 * bit, 1)
        down = pltpu.roll(pltpu.roll(x, bit, 0), 128 - 16 * bit, 1)
        x = jnp.where(s == c, x, jnp.where(c == 1, up, down))
    both = pltpu.roll(pltpu.roll(x, 4, 0), 64, 1)
    return jnp.where(sub_bit(4) == chunk // 4, x, both)


def split(x):
    hi = x.astype(jnp.bfloat16)
    lo = (x - hi.astype(jnp.float32)).astype(jnp.bfloat16)
    return hi, lo


def product(lhs, weights):
    hi, lo = split(lhs)
    full = jnp.dot(hi, weights, preferred_element_type=jnp.float32)
    rest = jnp.dot(lo, weights, preferred_element_type=jnp.float32)
    return full[:, :128] + (full[:, 128:] + (rest[:, :128] + rest[:, 128:]))


def body(
    n_wide, n_narrow,
    slot_ref, design_ref, tiles_ref, holes_ref, squeeze_ref, force_ref,
    pressure_ref, sens_ref,
    ext, blocks, curve, wf, wb, sums, st, st_l, st_r, k_l, k_r,
    cond, dens, wn, ws, ww, we, src, ping, pong,
    raw, raw_holes, out, send, recv, here_sem,
):
    w, n = lax.axis_index("wide"), lax.axis_index("narrow")
    owners = n_wide * n_narrow
    me = w * n_narrow + n
    after = lax.rem(me + 1, owners)
    before = lax.rem(me + owners - 1, owners)
    nxt = (after // n_narrow, lax.rem(after, n_narrow))
    prv = (before // n_narrow, lax.rem(before, n_narrow))
    up = (lax.rem(w + n_wide - 1, n_wide), n)
    down = (lax.rem(w + 1, n_wide), n)
    left = (w, lax.rem(n + n_narrow - 1, n_narrow))
    right = (w, lax.rem(n + 1, n_narrow))
    has_up, has_down = w > 0, w < n_wide - 1
    has_left, has_right = n > 0, n < n_narrow - 1

    loads = [
        pltpu.make_async_copy(squeeze_ref, raw.at[0], here_sem.at[0]),
        pltpu.make_async_copy(force_ref, raw.at[1], here_sem.at[1]),
        pltpu.make_async_copy(holes_ref, raw_holes, here_sem.at[2]),
        pltpu.make_async_copy(design_ref, ext.at[pl.ds(SENT, SLOTS)], here_sem.at[3]),
    ]
    for load in loads:
        load.start()

    barrier = pltpu.get_barrier_semaphore()
    pl.semaphore_signal(barrier, inc=1, device_id=nxt, device_id_type=MESH)
    pl.semaphore_signal(barrier, inc=1, device_id=prv, device_id_type=MESH)
    for there, device in ((has_up, up), (has_down, down), (has_left, left), (has_right, right)):
        @pl.when(there)
        def _():
            pl.semaphore_signal(barrier, inc=1, device_id=device, device_id_type=MESH)
    expected = 2 + sum(jnp.where(t, 1, 0) for t in (has_up, has_down, has_left, has_right))
    pl.semaphore_wait(barrier, expected)

    def remote(which, src_ref, dst_ref, device):
        return pltpu.make_async_remote_copy(
            src_ref=src_ref, dst_ref=dst_ref,
            send_sem=send.at[which], recv_sem=recv.at[which],
            device_id=device, device_id_type=MESH,
        )

    tile_rows = pl.ds(RIM, ROWS)
    top_rows, low_rows = pl.ds(RIM, RIM), pl.ds(ROWS, RIM)
    above_rows, below_rows = pl.ds(0, RIM), pl.ds(RIM + ROWS, RIM)
    st_top, st_low = pl.ds(RIM, DEEP), pl.ds(RIM + ROWS - DEEP, DEEP)
    st_above, st_below = pl.ds(RIM - DEEP, DEEP), pl.ds(RIM + ROWS, DEEP)
    design_copy = remote(DESIGN, design_ref.at[pl.ds(SLOTS - SENT, SENT)], ext.at[pl.ds(0, SENT)], nxt)
    st_left = remote(ST_L, st.at[:, 0, tile_rows], st_r, left)
    st_right = remote(ST_R, st.at[:, STRIPS - 1, tile_rows], st_l, right)
    st_up = remote(ST_U, st.at[:, :, st_top], st.at[:, :, st_below], up)
    st_down = remote(ST_D, st.at[:, :, st_low], st.at[:, :, st_above], down)
    k_left = remote(K_L, cond.at[0, tile_rows], k_r, left)
    k_right = remote(K_R, cond.at[STRIPS - 1, tile_rows], k_l, right)

    def k_rows(c, strips):
        return (
            remote(K_U + c, cond.at[strips, top_rows], cond.at[strips, below_rows], up), has_up,
            remote(K_D + c, cond.at[strips, low_rows], cond.at[strips, above_rows], down), has_down,
        )

    k_corners = k_rows(GROUPS, pl.ds(STRIPS, 1))

    def start_pair(first, has_first, second, has_second):
        pl.when(has_first)(first.start)
        pl.when(has_second)(second.start)

    def wait_pair(first, has_first, second, has_second):
        pl.when(has_first)(first.wait_send)
        pl.when(has_second)(second.wait_send)
        pl.when(has_second)(first.wait_recv)
        pl.when(has_first)(second.wait_recv)

    design_copy.start()

    for load in loads[:3]:
        load.wait()
    for g in range(STRIPS):
        cols = pl.ds(g * 128, 128)
        st[0, g, tile_rows, :] = raw[0, :, cols]
        st[1, g, tile_rows, :] = raw[1, :, cols]
        st[2, g, tile_rows, :] = jnp.where(raw_holes[:, cols] > 0, 0.0, 1.0).astype(jnp.float32)
    start_pair(st_left, has_left, st_right, has_right)

    blocks[...] = jnp.zeros(blocks.shape, jnp.float32)
    for k in range(5):
        tile = tiles_ref[k]
        turned = tile.T
        rows = pl.ds(k * 128, 128)
        hi, lo = split(turned)
        wf[rows, pl.ds(0, 128)] = hi
        wf[rows, pl.ds(128, 128)] = lo
        hi, lo = split(tile)
        wb[rows, pl.ds(0, 128)] = hi
        wb[rows, pl.ds(128, 128)] = lo
        sums[pl.ds(k, 1), :] = jnp.sum(turned, axis=0, keepdims=True)

    for there, value in ((has_left, st_l), (has_right, st_r)):
        @pl.when(jnp.logical_not(there))
        def _():
            value[...] = jnp.zeros(value.shape, jnp.float32)
    for there, value in ((has_left, k_l), (has_right, k_r)):
        @pl.when(jnp.logical_not(there))
        def _():
            value[...] = jnp.zeros(value.shape, jnp.float32)
    for there, rows in ((has_up, above_rows), (has_down, below_rows)):
        @pl.when(jnp.logical_not(there))
        def _():
            st[:, :, rows, :] = jnp.zeros((3, WIDE, RIM, 128), jnp.float32)
            cond[:, rows, :] = jnp.zeros((WIDE, RIM, 128), jnp.float32)

    wait_pair(st_left, has_left, st_right, has_right)
    lane = lax.broadcasted_iota(jnp.int32, (ROWS, 128), 1)
    for q in range(3):
        st[q, STRIPS, tile_rows, :] = jnp.where(lane < 64, st_r[q], st_l[q])
    start_pair(st_up, has_up, st_down, has_down)

    first = slot_ref[0]
    block_row, block_col = (first // 128) % 16, first % 128
    stagger = (block_col // 16) * 256
    for level in range(4):
        stagger = stagger + (block_col // 2**level) % 2 * 4**level
        stagger = stagger + (block_row // 2**level) % 2 * (2 * 4**level)

    loads[3].wait()
    design_copy.wait()
    offset = SENT - stagger

    def place(c, _):
        group = ext[pl.ds(offset + c * GROUP, GROUP), :]
        for (row, half), value in curve_to_rows(group).items():
            at = pl.multiple_of(8 + 16 * c + 8 * half, 8)
            blocks[1 + row, pl.ds(at, 8), :] = value
        return 0

    lax.fori_loop(0, GROUPS, place, 0)

    def near(c):
        def take(row, col):
            return blocks[pl.ds(1 + row, 16), pl.ds(8 + 16 * c + col, 16), :].reshape(GROUP, 128)
        return take

    def denominator(c, width, count):
        row = lax.broadcasted_iota(jnp.int32, (16, width, 128), 0)
        col = lax.broadcasted_iota(jnp.int32, (16, width, 128), 1) + c * width
        total = jnp.broadcast_to(sums[pl.ds(0, 1), :].reshape(1, 1, 128), row.shape)
        inside = (row > 0, row < 15, col > 0, col < 127)
        for k in range(4):
            total = total + jnp.where(inside[k], sums[pl.ds(k + 1, 1), :].reshape(1, 1, 128), 0.0)
        return total.reshape(count, 128)

    def forward(index, _):
        c = lax.rem(index * (GROUPS - 1), GROUPS)
        take = near(c)
        lhs = jnp.concatenate([take(0, 0), take(-1, 0), take(1, 0), take(0, -1), take(0, 1)], axis=1)
        filtered = product(lhs, wf[...]) / denominator(c, 16, GROUP)
        for row in range(16):
            for half in range(2):
                at = row * 16 + 8 * half
                film = flip_block(filtered[at : at + 8])
                dens[2 * c + half, pl.ds(row * 8, 8), :] = film
                cond[2 * c + half, pl.ds(RIM + row * 8, 8), :] = (
                    COND_FLOOR + (1.0 - COND_FLOOR) * film * film * film
                )
        start_pair(*k_rows(c, pl.ds(2 * c, 2)))
        pl.when((index == 0) & has_left)(k_left.start)
        pl.when((index == 1) & has_right)(k_right.start)
        return 0

    lax.fori_loop(0, GROUPS, forward, 0)
    wait_pair(k_left, has_left, k_right, has_right)
    cond[STRIPS, tile_rows, :] = jnp.where(lane < 64, k_r[...], k_l[...])
    start_pair(*k_corners)

    lane8 = lax.broadcasted_iota(jnp.int32, (8, 128), 1)

    def sides(row):
        out = []
        for g in range(WIDE):
            west = pltpu.roll(jnp.where(lane8 == 127, row[g - 1], row[g]), 1, 1)
            east = pltpu.roll(jnp.where(lane8 == 0, row[(g + 1) % WIDE], row[g]), 127, 1)
            out.append((west, east))
        return out

    def coefficients(step, _):
        r = pl.multiple_of(step * 8, 8)
        here = [cond[g, pl.ds(r, 8), :] for g in range(WIDE)]
        beside = sides(here)
        for g in range(WIDE):
            k = here[g]
            north = 0.5 * (k + cond[g, pl.ds(r - 1, 8), :])
            south = 0.5 * (k + cond[g, pl.ds(r + 1, 8), :])
            west = 0.5 * (k + beside[g][0])
            east = 0.5 * (k + beside[g][1])
            inverse = 1.0 / (north + south + west + east + SQUEEZE_DAMPING)
            solid = st[2, g, pl.ds(r, 8), :] > 0.5
            for ref, face in ((wn, north), (ws, south), (ww, west), (we, east)):
                ref[g, pl.ds(r, 8), :] = jnp.where(solid, face * inverse, 0.0)
            for q in range(2):
                value = jnp.where(solid, st[q, g, pl.ds(r, 8), :] * inverse, 0.0)
                src[q, g, pl.ds(r, 8), :] = value
                ping[q, g, pl.ds(r, 8), :] = value
        return 0

    lax.fori_loop(4, 18, coefficients, 0)
    wait_pair(st_up, has_up, st_down, has_down)

    def rows_arrived(c, _):
        wait_pair(*k_rows(c, pl.ds(2 * c, 2)))
        return 0

    lax.fori_loop(0, GROUPS, rows_arrived, 0)
    wait_pair(*k_corners)
    lax.fori_loop(1, 4, coefficients, 0)
    lax.fori_loop(18, 21, coefficients, 0)

    def sweep(old, new, first_step, last_step):
        def row_of_strips(r, q):
            rows = pl.ds(r, 8)
            here = {g: old[q, g, rows, :] for g in (STRIPS, 0)}
            for g in range(WIDE):
                after = (g + 1) % WIDE
                if after not in here:
                    here[after] = old[q, after, rows, :]
                west = pltpu.roll(jnp.where(lane8 == 127, here[(g + STRIPS) % WIDE], here[g]), 1, 1)
                east = pltpu.roll(jnp.where(lane8 == 0, here[after], here[g]), 127, 1)
                north = old[q, g, pl.ds(r - 1, 8), :]
                south = old[q, g, pl.ds(r + 1, 8), :]
                new[q, g, rows, :] = (
                    src[q, g, rows, :] + wn[g, rows, :] * north + ws[g, rows, :] * south
                ) + (ww[g, rows, :] * west + we[g, rows, :] * east)

        def pair(step, _):
            for half in range(2):
                r = pl.multiple_of((first_step + 2 * step + half) * 8, 8)
                for q in range(2):
                    row_of_strips(r, q)
            return 0

        lax.fori_loop(0, (last_step - first_step) // 2, pair, 0)

    def two_deep(_, carry):
        sweep(ping, pong, 1, 21)
        sweep(pong, ping, 1, 21)
        return carry

    def two_shallow(_, carry):
        sweep(pong, ping, 2, 20)
        sweep(ping, pong, 2, 20)
        return carry

    lax.fori_loop(0, 3, two_deep, 0)
    sweep(ping, pong, 1, 21)
    lax.fori_loop(0, (SWEEPS - 8) // 2, two_shallow, 0)

    def gradient(g):
        summed = jnp.zeros((ROWS, 128), jnp.float32)
        p = pong[0, g, tile_rows, :]
        a = pong[1, g, tile_rows, :]
        out[:, pl.ds(g * 128 if isinstance(g, int) else pl.multiple_of(g * 128, 128), 128)] = p
        for shift in (RIM - 1, RIM + 1):
            rows = pl.ds(shift, ROWS)
            summed = summed + (a - pong[1, g, rows, :]) * (p - pong[0, g, rows, :])
        west, east = lax.rem(g + STRIPS, WIDE), g + 1
        for edge, strip, turn in ((127, west, 1), (0, east, 127)):
            pn = pltpu.roll(jnp.where(lane == edge, pong[0, strip, tile_rows, :], p), turn, 1)
            an = pltpu.roll(jnp.where(lane == edge, pong[1, strip, tile_rows, :], a), turn, 1)
            summed = summed + (a - an) * (p - pn)
        density = dens[g]
        sens = -0.5 * summed * (3.0 * (1.0 - COND_FLOOR)) * density * density
        scale = denominator(g, 8, ROWS)
        at = 8 + 8 * g if isinstance(g, int) else pl.multiple_of(8 + 8 * g, 8)
        for row in range(16):
            part = slice(row * 8, row * 8 + 8)
            blocks[1 + row, pl.ds(at, 8), :] = flip_block(sens[part]) / scale[part]

    def back_copy(c):
        return remote(BACK + c, curve.at[pl.ds(c * GROUP, GROUP)], curve.at[pl.ds(SLOTS + c * GROUP, GROUP)], prv)

    def backward(c):
        take = near(c)
        lhs = jnp.concatenate([take(0, 0), take(1, 0), take(-1, 0), take(0, 1), take(0, -1)], axis=1)
        for v, value in enumerate(rows_to_curve(product(lhs, wb[...]))):
            at = c * GROUP + 8 * v
            if not isinstance(at, int):
                at = pl.multiple_of(at, 8)
            curve[pl.ds(at, 8), :] = value

    def back(c, _):
        gradient(2 * c + 1)
        gradient(2 * c + 2)
        backward(c)
        back_copy(c).start()
        return 0

    gradient(0)
    lax.fori_loop(0, SENT_GROUPS, back, 0)
    gradient(13)
    gradient(14)
    backward(6)
    gradient(15)
    pressure_copy = pltpu.make_async_copy(out, pressure_ref, here_sem.at[0])
    pressure_copy.start()
    backward(7)

    def give(c):
        at = c * GROUP
        sens_ref[pl.ds(at, GROUP), :] = curve[pl.ds(stagger + at, GROUP), :]

    for c in range(SENT_GROUPS):
        back_copy(c).wait()
    for c in range(GROUPS):
        give(c)
    pressure_copy.wait()


def solution(mesh):
    n_wide, n_narrow = mesh.shape["wide"], mesh.shape["narrow"]
    f32, bf16 = jnp.float32, jnp.bfloat16
    vmem = pl.BlockSpec(memory_space=pltpu.VMEM)
    anywhere = pl.BlockSpec(memory_space=pl.ANY)

    def local(design, filter_tiles, filter_cols, slot_block, holes, squeeze_source, force_weight):
        strips = (WIDE, TALL, 128)
        return pl.pallas_call(
            functools.partial(body, n_wide, n_narrow),
            out_shape=(
                jax.ShapeDtypeStruct(holes.shape, f32),
                jax.ShapeDtypeStruct(design.shape, f32),
            ),
            in_specs=[pl.BlockSpec(memory_space=pltpu.SMEM), anywhere, vmem] + [anywhere] * 3,
            out_specs=(anywhere, vmem),
            scratch_shapes=[
                pltpu.VMEM((SENT + SLOTS + 8, 128), f32),
                pltpu.VMEM((18, 144, 128), f32),
                pltpu.VMEM((SENT + SLOTS + 8, 128), f32),
                pltpu.VMEM((640, 256), bf16),
                pltpu.VMEM((640, 256), bf16),
                pltpu.VMEM((8, 128), f32),
                pltpu.VMEM((3,) + strips, f32),
                pltpu.VMEM((3, ROWS, 128), f32),
                pltpu.VMEM((3, ROWS, 128), f32),
                pltpu.VMEM((ROWS, 128), f32),
                pltpu.VMEM((ROWS, 128), f32),
                pltpu.VMEM(strips, f32),
                pltpu.VMEM((STRIPS, ROWS, 128), f32),
                pltpu.VMEM(strips, f32),
                pltpu.VMEM(strips, f32),
                pltpu.VMEM(strips, f32),
                pltpu.VMEM(strips, f32),
                pltpu.VMEM((2,) + strips, f32),
                pltpu.VMEM((2,) + strips, f32),
                pltpu.VMEM((2,) + strips, f32),
                pltpu.VMEM((2,) + holes.shape, f32),
                pltpu.VMEM(holes.shape, jnp.int32),
                pltpu.VMEM(holes.shape, f32),
                pltpu.SemaphoreType.DMA((COPIES,)),
                pltpu.SemaphoreType.DMA((COPIES,)),
                pltpu.SemaphoreType.DMA((4,)),
            ],
            compiler_params=pltpu.CompilerParams(
                collective_id=0, has_side_effects=True, vmem_limit_bytes=56 * 2**20
            ),
        )(slot_block, design, filter_tiles, holes, squeeze_source, force_weight)

    placed = (
        P(("wide", "narrow"), None),
        P(),
        P(("wide", "narrow"), None),
        P(("wide", "narrow")),
        P("wide", "narrow"),
        P("wide", "narrow"),
        P("wide", "narrow"),
    )
    return jax.shard_map(
        local,
        mesh=mesh,
        in_specs=placed,
        out_specs=(P("wide", "narrow"), P(("wide", "narrow"), None)),
        check_vma=False,
    )
```

```python
import functools

import jax
import jax.numpy as jnp
from jax import lax
from jax.experimental import pallas as pl
from jax.experimental.pallas import tpu as pltpu
from jax.sharding import PartitionSpec as P

SWEEPS = 16
COND_FLOOR = 0.01
SQUEEZE_DAMPING = 0.25
MESH = pl.DeviceIdType.MESH

SLOTS = 2048
RIM = 24
ROWS = 128
TALL = ROWS + 2 * RIM
STRIPS = 16
WIDE = STRIPS + 1
SENT = 1536
GROUP = 256
GROUPS = SLOTS // GROUP
SENT_GROUPS = SENT // GROUP

DEEP = 16
DESIGN, ST_L, ST_R, ST_U, ST_D, K_L, K_R = range(7)
K_U = 7
K_D = K_U + GROUPS + 1
BACK = K_D + GROUPS + 1
COPIES = BACK + SENT_GROUPS


def sub_bit(bit):
    return (lax.broadcasted_iota(jnp.int32, (8, 128), 0) // bit) % 2


def swap_middle(x):
    b1, b2 = sub_bit(2), sub_bit(4)
    moved = jnp.where(b1 == 1, pltpu.roll(x, 6, 0), pltpu.roll(x, 2, 0))
    return jnp.where(b1 == b2, x, moved)


def curve_to_rows(group):
    low = sub_bit(2) == 0
    out = {}
    for r3 in range(2):
        for c3 in range(2):
            for r2 in range(2):
                for r1 in range(2):
                    at = 8 * (r1 + 4 * r2 + 8 * c3 + 16 * r3)
                    a, b = group[at : at + 8], group[at + 16 : at + 24]
                    row = 2 * r1 + 4 * r2 + 8 * r3
                    even = jnp.where(low, a, pltpu.roll(b, 2, 0))
                    odd = jnp.where(low, pltpu.roll(a, 6, 0), b)
                    out[row, c3] = swap_middle(even)
                    out[row + 1, c3] = swap_middle(odd)
    return out


def rows_to_curve(group):
    low = sub_bit(2) == 0
    out = [None] * 32
    for r3 in range(2):
        for c3 in range(2):
            for r2 in range(2):
                for r1 in range(2):
                    row = 2 * r1 + 4 * r2 + 8 * r3
                    at = row * 16 + 8 * c3
                    even = swap_middle(group[at : at + 8])
                    odd = swap_middle(group[at + 16 : at + 24])
                    v = r1 + 4 * r2 + 8 * c3 + 16 * r3
                    out[v] = jnp.where(low, even, pltpu.roll(odd, 2, 0))
                    out[v + 2] = jnp.where(low, pltpu.roll(even, 6, 0), odd)
    return out


def flip_block(x):
    chunk = lax.broadcasted_iota(jnp.int32, (8, 128), 1) // 16
    for bit in (1, 2):
        s, c = sub_bit(bit), (chunk // bit) % 2
        up = pltpu.roll(pltpu.roll(x, 8 - bit, 0), 16 * bit, 1)
        down = pltpu.roll(pltpu.roll(x, bit, 0), 128 - 16 * bit, 1)
        x = jnp.where(s == c, x, jnp.where(c == 1, up, down))
    both = pltpu.roll(pltpu.roll(x, 4, 0), 64, 1)
    return jnp.where(sub_bit(4) == chunk // 4, x, both)


def split(x):
    hi = x.astype(jnp.bfloat16)
    lo = (x - hi.astype(jnp.float32)).astype(jnp.bfloat16)
    return hi, lo


def product(lhs, weights):
    hi, lo = split(lhs)
    full = jnp.dot(hi, weights, preferred_element_type=jnp.float32)
    rest = jnp.dot(lo, weights, preferred_element_type=jnp.float32)
    return full[:, :128] + (full[:, 128:] + (rest[:, :128] + rest[:, 128:]))


def body(
    n_wide, n_narrow,
    slot_ref, design_ref, tiles_ref, holes_ref, squeeze_ref, force_ref,
    pressure_ref, sens_ref,
    ext, blocks, curve, wf, wb, sums, st, st_l, st_r, k_l, k_r,
    cond, dens, wn, ws, ww, we, src, ping, pong,
    raw, raw_holes, out, send, recv, here_sem,
):
    w, n = lax.axis_index("wide"), lax.axis_index("narrow")
    owners = n_wide * n_narrow
    me = w * n_narrow + n
    after = lax.rem(me + 1, owners)
    before = lax.rem(me + owners - 1, owners)
    nxt = (after // n_narrow, lax.rem(after, n_narrow))
    prv = (before // n_narrow, lax.rem(before, n_narrow))
    up = (lax.rem(w + n_wide - 1, n_wide), n)
    down = (lax.rem(w + 1, n_wide), n)
    left = (w, lax.rem(n + n_narrow - 1, n_narrow))
    right = (w, lax.rem(n + 1, n_narrow))
    has_up, has_down = w > 0, w < n_wide - 1
    has_left, has_right = n > 0, n < n_narrow - 1

    loads = [
        pltpu.make_async_copy(squeeze_ref, raw.at[0], here_sem.at[0]),
        pltpu.make_async_copy(force_ref, raw.at[1], here_sem.at[1]),
        pltpu.make_async_copy(holes_ref, raw_holes, here_sem.at[2]),
        pltpu.make_async_copy(design_ref, ext.at[pl.ds(SENT, SLOTS)], here_sem.at[3]),
    ]
    for load in loads:
        load.start()

    barrier = pltpu.get_barrier_semaphore()
    pl.semaphore_signal(barrier, inc=1, device_id=nxt, device_id_type=MESH)
    pl.semaphore_signal(barrier, inc=1, device_id=prv, device_id_type=MESH)
    for there, device in ((has_up, up), (has_down, down), (has_left, left), (has_right, right)):
        @pl.when(there)
        def _():
            pl.semaphore_signal(barrier, inc=1, device_id=device, device_id_type=MESH)
    expected = 2 + sum(jnp.where(t, 1, 0) for t in (has_up, has_down, has_left, has_right))
    pl.semaphore_wait(barrier, expected)

    def remote(which, src_ref, dst_ref, device):
        return pltpu.make_async_remote_copy(
            src_ref=src_ref, dst_ref=dst_ref,
            send_sem=send.at[which], recv_sem=recv.at[which],
            device_id=device, device_id_type=MESH,
        )

    tile_rows = pl.ds(RIM, ROWS)
    k_top, k_low = pl.ds(RIM, DEEP + 1), pl.ds(RIM + ROWS - DEEP - 1, DEEP + 1)
    k_above, k_below = pl.ds(RIM - DEEP - 1, DEEP + 1), pl.ds(RIM + ROWS, DEEP + 1)
    above_rows, below_rows = pl.ds(0, RIM), pl.ds(RIM + ROWS, RIM)
    st_top, st_low = pl.ds(RIM, DEEP), pl.ds(RIM + ROWS - DEEP, DEEP)
    st_above, st_below = pl.ds(RIM - DEEP, DEEP), pl.ds(RIM + ROWS, DEEP)
    design_copy = remote(DESIGN, design_ref.at[pl.ds(SLOTS - SENT, SENT)], ext.at[pl.ds(0, SENT)], nxt)
    st_left = remote(ST_L, st.at[:, 0, tile_rows], st_r, left)
    st_right = remote(ST_R, st.at[:, STRIPS - 1, tile_rows], st_l, right)
    st_up = remote(ST_U, st.at[:, :, st_top], st.at[:, :, st_below], up)
    st_down = remote(ST_D, st.at[:, :, st_low], st.at[:, :, st_above], down)
    k_left = remote(K_L, cond.at[0, tile_rows], k_r, left)
    k_right = remote(K_R, cond.at[STRIPS - 1, tile_rows], k_l, right)

    def k_rows(c, strips):
        return (
            remote(K_U + c, cond.at[strips, k_top], cond.at[strips, k_below], up), has_up,
            remote(K_D + c, cond.at[strips, k_low], cond.at[strips, k_above], down), has_down,
        )

    k_corners = k_rows(GROUPS, pl.ds(STRIPS, 1))

    def start_pair(first, has_first, second, has_second):
        pl.when(has_first)(first.start)
        pl.when(has_second)(second.start)

    def wait_pair(first, has_first, second, has_second):
        pl.when(has_first)(first.wait_send)
        pl.when(has_second)(second.wait_send)
        pl.when(has_second)(first.wait_recv)
        pl.when(has_first)(second.wait_recv)

    design_copy.start()

    for load in loads[:3]:
        load.wait()
    for g in range(STRIPS):
        cols = pl.ds(g * 128, 128)
        solid = raw_holes[:, cols] <= 0
        st[0, g, tile_rows, :] = jnp.where(solid, raw[0, :, cols], 0.0)
        st[1, g, tile_rows, :] = jnp.where(solid, raw[1, :, cols], 0.0)
    start_pair(st_left, has_left, st_right, has_right)

    blocks[...] = jnp.zeros(blocks.shape, jnp.float32)
    for k in range(5):
        tile = tiles_ref[k]
        turned = tile.T
        rows = pl.ds(k * 128, 128)
        hi, lo = split(turned)
        wf[rows, pl.ds(0, 128)] = hi
        wf[rows, pl.ds(128, 128)] = lo
        hi, lo = split(tile)
        wb[rows, pl.ds(0, 128)] = hi
        wb[rows, pl.ds(128, 128)] = lo
        sums[pl.ds(k, 1), :] = jnp.sum(turned, axis=0, keepdims=True)

    for there, value in ((has_left, st_l), (has_right, st_r)):
        @pl.when(jnp.logical_not(there))
        def _():
            value[...] = jnp.zeros(value.shape, jnp.float32)
    for there, value in ((has_left, k_l), (has_right, k_r)):
        @pl.when(jnp.logical_not(there))
        def _():
            value[...] = jnp.zeros(value.shape, jnp.float32)
    for there, rows in ((has_up, above_rows), (has_down, below_rows)):
        @pl.when(jnp.logical_not(there))
        def _():
            st[:, :, rows, :] = jnp.zeros((2, WIDE, RIM, 128), jnp.float32)
            cond[:, rows, :] = jnp.zeros((WIDE, RIM, 128), jnp.float32)

    wait_pair(st_left, has_left, st_right, has_right)
    lane = lax.broadcasted_iota(jnp.int32, (ROWS, 128), 1)
    for q in range(2):
        st[q, STRIPS, tile_rows, :] = jnp.where(lane < 64, st_r[q], st_l[q])
    start_pair(st_up, has_up, st_down, has_down)

    first = slot_ref[0]
    block_row, block_col = (first // 128) % 16, first % 128
    stagger = (block_col // 16) * 256
    for level in range(4):
        stagger = stagger + (block_col // 2**level) % 2 * 4**level
        stagger = stagger + (block_row // 2**level) % 2 * (2 * 4**level)

    loads[3].wait()
    design_copy.wait()
    offset = SENT - stagger

    def place(c, _):
        group = ext[pl.ds(offset + c * GROUP, GROUP), :]
        for (row, half), value in curve_to_rows(group).items():
            at = pl.multiple_of(8 + 16 * c + 8 * half, 8)
            blocks[1 + row, pl.ds(at, 8), :] = value
        return 0

    lax.fori_loop(0, GROUPS, place, 0)

    def near(c):
        def take(row, col):
            return blocks[pl.ds(1 + row, 16), pl.ds(8 + 16 * c + col, 16), :].reshape(GROUP, 128)
        return take

    def denominator(c, width, count):
        row = lax.broadcasted_iota(jnp.int32, (16, width, 128), 0)
        col = lax.broadcasted_iota(jnp.int32, (16, width, 128), 1) + c * width
        total = jnp.broadcast_to(sums[pl.ds(0, 1), :].reshape(1, 1, 128), row.shape)
        inside = (row > 0, row < 15, col > 0, col < 127)
        for k in range(4):
            total = total + jnp.where(inside[k], sums[pl.ds(k + 1, 1), :].reshape(1, 1, 128), 0.0)
        return total.reshape(count, 128)

    def forward(index, _):
        c = lax.rem(index * (GROUPS - 1), GROUPS)
        take = near(c)
        lhs = jnp.concatenate([take(0, 0), take(-1, 0), take(1, 0), take(0, -1), take(0, 1)], axis=1)
        filtered = product(lhs, wf[...]) / denominator(c, 16, GROUP)
        for row in range(16):
            for half in range(2):
                at = row * 16 + 8 * half
                film = flip_block(filtered[at : at + 8])
                dens[2 * c + half, pl.ds(row * 8, 8), :] = film
                cond[2 * c + half, pl.ds(RIM + row * 8, 8), :] = (
                    COND_FLOOR + (1.0 - COND_FLOOR) * film * film * film
                )
        start_pair(*k_rows(c, pl.ds(2 * c, 2)))
        pl.when((index == 0) & has_left)(k_left.start)
        pl.when((index == 1) & has_right)(k_right.start)
        return 0

    lax.fori_loop(0, GROUPS, forward, 0)
    wait_pair(k_left, has_left, k_right, has_right)
    cond[STRIPS, tile_rows, :] = jnp.where(lane < 64, k_r[...], k_l[...])
    start_pair(*k_corners)

    lane8 = lax.broadcasted_iota(jnp.int32, (8, 128), 1)

    def sides(row):
        out = []
        for g in range(WIDE):
            west = pltpu.roll(jnp.where(lane8 == 127, row[g - 1], row[g]), 1, 1)
            east = pltpu.roll(jnp.where(lane8 == 0, row[(g + 1) % WIDE], row[g]), 127, 1)
            out.append((west, east))
        return out

    def coefficients(step, _):
        r = pl.multiple_of(step * 8, 8)
        here = [cond[g, pl.ds(r, 8), :] for g in range(WIDE)]
        beside = sides(here)
        for g in range(WIDE):
            k = here[g]
            north = 0.5 * (k + cond[g, pl.ds(r - 1, 8), :])
            south = 0.5 * (k + cond[g, pl.ds(r + 1, 8), :])
            west = 0.5 * (k + beside[g][0])
            east = 0.5 * (k + beside[g][1])
            inverse = 1.0 / (north + south + west + east + SQUEEZE_DAMPING)
            solid = st[1, g, pl.ds(r, 8), :] > 0.0
            for ref, face in ((wn, north), (ws, south), (ww, west), (we, east)):
                ref[g, pl.ds(r, 8), :] = jnp.where(solid, face * inverse, 0.0)
            for q in range(2):
                value = st[q, g, pl.ds(r, 8), :] * inverse
                src[q, g, pl.ds(r, 8), :] = value
                ping[q, g, pl.ds(r, 8), :] = value
        return 0

    lax.fori_loop(4, 18, coefficients, 0)
    wait_pair(st_up, has_up, st_down, has_down)

    def rows_arrived(c, _):
        wait_pair(*k_rows(c, pl.ds(2 * c, 2)))
        return 0

    lax.fori_loop(0, GROUPS, rows_arrived, 0)
    wait_pair(*k_corners)
    lax.fori_loop(1, 4, coefficients, 0)
    lax.fori_loop(18, 21, coefficients, 0)

    def sweep(old, new, first_step, last_step, unroll):
        def row_of_strips(r):
            rows = pl.ds(r, 8)
            here = {(q, g): old[q, g, rows, :] for q in range(2) for g in (STRIPS, 0)}
            for g in range(WIDE):
                before, after = (g + STRIPS) % WIDE, (g + 1) % WIDE
                faces = [ref[g, rows, :] for ref in (wn, ws, ww, we)]
                for q in range(2):
                    if (q, after) not in here:
                        here[q, after] = old[q, after, rows, :]
                    mine = here[q, g]
                    west = pltpu.roll(jnp.where(lane8 == 127, here[q, before], mine), 1, 1)
                    east = pltpu.roll(jnp.where(lane8 == 0, here[q, after], mine), 127, 1)
                    north = old[q, g, pl.ds(r - 1, 8), :]
                    south = old[q, g, pl.ds(r + 1, 8), :]
                    new[q, g, rows, :] = (
                        src[q, g, rows, :] + faces[0] * north + faces[1] * south
                    ) + (faces[2] * west + faces[3] * east)

        def several(step, _):
            for part in range(unroll):
                row_of_strips(pl.multiple_of((first_step + unroll * step + part) * 8, 8))
            return 0

        lax.fori_loop(0, (last_step - first_step) // unroll, several, 0)

    def two_deep(_, carry):
        sweep(ping, pong, 1, 21, 4)
        sweep(pong, ping, 1, 21, 4)
        return carry

    def two_shallow(_, carry):
        sweep(pong, ping, 2, 20, 3)
        sweep(ping, pong, 2, 20, 3)
        return carry

    lax.fori_loop(0, 3, two_deep, 0)
    sweep(ping, pong, 1, 21, 4)
    lax.fori_loop(0, (SWEEPS - 8) // 2, two_shallow, 0)

    def gradient(g):
        summed = jnp.zeros((ROWS, 128), jnp.float32)
        p = pong[0, g, tile_rows, :]
        a = pong[1, g, tile_rows, :]
        out[:, pl.ds(g * 128 if isinstance(g, int) else pl.multiple_of(g * 128, 128), 128)] = p
        for shift in (RIM - 1, RIM + 1):
            rows = pl.ds(shift, ROWS)
            summed = summed + (a - pong[1, g, rows, :]) * (p - pong[0, g, rows, :])
        west, east = lax.rem(g + STRIPS, WIDE), g + 1
        for edge, strip, turn in ((127, west, 1), (0, east, 127)):
            pn = pltpu.roll(jnp.where(lane == edge, pong[0, strip, tile_rows, :], p), turn, 1)
            an = pltpu.roll(jnp.where(lane == edge, pong[1, strip, tile_rows, :], a), turn, 1)
            summed = summed + (a - an) * (p - pn)
        density = dens[g]
        sens = -0.5 * summed * (3.0 * (1.0 - COND_FLOOR)) * density * density
        scale = denominator(g, 8, ROWS)
        at = 8 + 8 * g if isinstance(g, int) else pl.multiple_of(8 + 8 * g, 8)
        for row in range(16):
            part = slice(row * 8, row * 8 + 8)
            blocks[1 + row, pl.ds(at, 8), :] = flip_block(sens[part]) / scale[part]

    def back_copy(c):
        return remote(BACK + c, curve.at[pl.ds(c * GROUP, GROUP)], curve.at[pl.ds(SLOTS + c * GROUP, GROUP)], prv)

    def backward(c):
        take = near(c)
        lhs = jnp.concatenate([take(0, 0), take(1, 0), take(-1, 0), take(0, 1), take(0, -1)], axis=1)
        for v, value in enumerate(rows_to_curve(product(lhs, wb[...]))):
            at = c * GROUP + 8 * v
            if not isinstance(at, int):
                at = pl.multiple_of(at, 8)
            curve[pl.ds(at, 8), :] = value

    def back(c, _):
        gradient(2 * c + 1)
        gradient(2 * c + 2)
        backward(c)
        back_copy(c).start()
        return 0

    gradient(0)
    lax.fori_loop(0, SENT_GROUPS, back, 0)
    gradient(13)
    gradient(14)
    backward(6)
    gradient(15)
    pressure_copy = pltpu.make_async_copy(out, pressure_ref, here_sem.at[0])
    pressure_copy.start()
    backward(7)

    def give(c):
        at = c * GROUP
        sens_ref[pl.ds(at, GROUP), :] = curve[pl.ds(stagger + at, GROUP), :]

    for c in range(SENT_GROUPS):
        back_copy(c).wait()
    for c in range(GROUPS):
        give(c)
    pressure_copy.wait()


def solution(mesh):
    n_wide, n_narrow = mesh.shape["wide"], mesh.shape["narrow"]
    f32, bf16 = jnp.float32, jnp.bfloat16
    vmem = pl.BlockSpec(memory_space=pltpu.VMEM)
    anywhere = pl.BlockSpec(memory_space=pl.ANY)

    def local(design, filter_tiles, filter_cols, slot_block, holes, squeeze_source, force_weight):
        strips = (WIDE, TALL, 128)
        return pl.pallas_call(
            functools.partial(body, n_wide, n_narrow),
            out_shape=(
                jax.ShapeDtypeStruct(holes.shape, f32),
                jax.ShapeDtypeStruct(design.shape, f32),
            ),
            in_specs=[pl.BlockSpec(memory_space=pltpu.SMEM), anywhere, vmem] + [anywhere] * 3,
            out_specs=(anywhere, vmem),
            scratch_shapes=[
                pltpu.VMEM((SENT + SLOTS + 8, 128), f32),
                pltpu.VMEM((18, 144, 128), f32),
                pltpu.VMEM((SENT + SLOTS + 8, 128), f32),
                pltpu.VMEM((640, 256), bf16),
                pltpu.VMEM((640, 256), bf16),
                pltpu.VMEM((8, 128), f32),
                pltpu.VMEM((2,) + strips, f32),
                pltpu.VMEM((2, ROWS, 128), f32),
                pltpu.VMEM((2, ROWS, 128), f32),
                pltpu.VMEM((ROWS, 128), f32),
                pltpu.VMEM((ROWS, 128), f32),
                pltpu.VMEM(strips, f32),
                pltpu.VMEM((STRIPS, ROWS, 128), f32),
                pltpu.VMEM(strips, f32),
                pltpu.VMEM(strips, f32),
                pltpu.VMEM(strips, f32),
                pltpu.VMEM(strips, f32),
                pltpu.VMEM((2,) + strips, f32),
                pltpu.VMEM((2,) + strips, f32),
                pltpu.VMEM((2,) + strips, f32),
                pltpu.VMEM((2,) + holes.shape, f32),
                pltpu.VMEM(holes.shape, jnp.int32),
                pltpu.VMEM(holes.shape, f32),
                pltpu.SemaphoreType.DMA((COPIES,)),
                pltpu.SemaphoreType.DMA((COPIES,)),
                pltpu.SemaphoreType.DMA((4,)),
            ],
            compiler_params=pltpu.CompilerParams(
                collective_id=0, has_side_effects=True, vmem_limit_bytes=56 * 2**20
            ),
        )(slot_block, design, filter_tiles, holes, squeeze_source, force_weight)

    placed = (
        P(("wide", "narrow"), None),
        P(),
        P(("wide", "narrow"), None),
        P(("wide", "narrow")),
        P("wide", "narrow"),
        P("wide", "narrow"),
        P("wide", "narrow"),
    )
    return jax.shard_map(
        local,
        mesh=mesh,
        in_specs=placed,
        out_specs=(P("wide", "narrow"), P(("wide", "narrow"), None)),
        check_vma=False,
    )
```

```python
import functools

import jax
import jax.numpy as jnp
from jax import lax
from jax.experimental import pallas as pl
from jax.experimental.pallas import tpu as pltpu
from jax.sharding import PartitionSpec as P

SWEEPS = 16
COND_FLOOR = 0.01
SQUEEZE_DAMPING = 0.25
MESH = pl.DeviceIdType.MESH

SLOTS = 2048
RIM = 24
ROWS = 128
TALL = ROWS + 2 * RIM
STRIPS = 16
WIDE = STRIPS + 1
SENT = 1536
GROUP = 256
GROUPS = SLOTS // GROUP
SENT_GROUPS = SENT // GROUP

DEEP = 16
DESIGN, ST_L, ST_R, ST_U, ST_D, K_L, K_R = range(7)
K_U = 7
K_D = K_U + GROUPS + 1
BACK = K_D + GROUPS + 1
COPIES = BACK + SENT_GROUPS


def sub_bit(bit):
    return (lax.broadcasted_iota(jnp.int32, (8, 128), 0) // bit) % 2


def swap_middle(x):
    b1, b2 = sub_bit(2), sub_bit(4)
    moved = jnp.where(b1 == 1, pltpu.roll(x, 6, 0), pltpu.roll(x, 2, 0))
    return jnp.where(b1 == b2, x, moved)


def curve_to_rows(group):
    low = sub_bit(2) == 0
    out = {}
    for r3 in range(2):
        for c3 in range(2):
            for r2 in range(2):
                for r1 in range(2):
                    at = 8 * (r1 + 4 * r2 + 8 * c3 + 16 * r3)
                    a, b = group[at : at + 8], group[at + 16 : at + 24]
                    row = 2 * r1 + 4 * r2 + 8 * r3
                    even = jnp.where(low, a, pltpu.roll(b, 2, 0))
                    odd = jnp.where(low, pltpu.roll(a, 6, 0), b)
                    out[row, c3] = swap_middle(even)
                    out[row + 1, c3] = swap_middle(odd)
    return out


def rows_to_curve(group):
    low = sub_bit(2) == 0
    out = [None] * 32
    for r3 in range(2):
        for c3 in range(2):
            for r2 in range(2):
                for r1 in range(2):
                    row = 2 * r1 + 4 * r2 + 8 * r3
                    at = row * 16 + 8 * c3
                    even = swap_middle(group[at : at + 8])
                    odd = swap_middle(group[at + 16 : at + 24])
                    v = r1 + 4 * r2 + 8 * c3 + 16 * r3
                    out[v] = jnp.where(low, even, pltpu.roll(odd, 2, 0))
                    out[v + 2] = jnp.where(low, pltpu.roll(even, 6, 0), odd)
    return out


def flip_block(x):
    chunk = lax.broadcasted_iota(jnp.int32, (8, 128), 1) // 16
    for bit in (1, 2):
        s, c = sub_bit(bit), (chunk // bit) % 2
        up = pltpu.roll(pltpu.roll(x, 8 - bit, 0), 16 * bit, 1)
        down = pltpu.roll(pltpu.roll(x, bit, 0), 128 - 16 * bit, 1)
        x = jnp.where(s == c, x, jnp.where(c == 1, up, down))
    both = pltpu.roll(pltpu.roll(x, 4, 0), 64, 1)
    return jnp.where(sub_bit(4) == chunk // 4, x, both)


def split(x):
    hi = x.astype(jnp.bfloat16)
    lo = (x - hi.astype(jnp.float32)).astype(jnp.bfloat16)
    return hi, lo


def product(lhs, weights):
    hi, lo = split(lhs)
    full = jnp.dot(hi, weights, preferred_element_type=jnp.float32)
    rest = jnp.dot(lo, weights, preferred_element_type=jnp.float32)
    return full[:, :128] + (full[:, 128:] + (rest[:, :128] + rest[:, 128:]))


def body(
    n_wide, n_narrow,
    slot_ref, design_ref, tiles_ref, holes_ref, squeeze_ref, force_ref,
    pressure_ref, sens_ref,
    ext, blocks, curve, wf, wb, sums, st, st_l, st_r, k_l, k_r,
    cond, dens, wn, ws, ww, we, src, ping, pong,
    raw, raw_holes, out, send, recv, here_sem,
):
    w, n = lax.axis_index("wide"), lax.axis_index("narrow")
    owners = n_wide * n_narrow
    me = w * n_narrow + n
    after = lax.rem(me + 1, owners)
    before = lax.rem(me + owners - 1, owners)
    nxt = (after // n_narrow, lax.rem(after, n_narrow))
    prv = (before // n_narrow, lax.rem(before, n_narrow))
    up = (lax.rem(w + n_wide - 1, n_wide), n)
    down = (lax.rem(w + 1, n_wide), n)
    left = (w, lax.rem(n + n_narrow - 1, n_narrow))
    right = (w, lax.rem(n + 1, n_narrow))
    has_up, has_down = w > 0, w < n_wide - 1
    has_left, has_right = n > 0, n < n_narrow - 1

    loads = [
        pltpu.make_async_copy(squeeze_ref, raw.at[0], here_sem.at[0]),
        pltpu.make_async_copy(force_ref, raw.at[1], here_sem.at[1]),
        pltpu.make_async_copy(holes_ref, raw_holes, here_sem.at[2]),
        pltpu.make_async_copy(design_ref, ext.at[pl.ds(SENT, SLOTS)], here_sem.at[3]),
    ]
    for load in loads:
        load.start()

    barrier = pltpu.get_barrier_semaphore()
    pl.semaphore_signal(barrier, inc=1, device_id=nxt, device_id_type=MESH)
    pl.semaphore_signal(barrier, inc=1, device_id=prv, device_id_type=MESH)
    for there, device in ((has_up, up), (has_down, down), (has_left, left), (has_right, right)):
        @pl.when(there)
        def _():
            pl.semaphore_signal(barrier, inc=1, device_id=device, device_id_type=MESH)
    expected = 2 + sum(jnp.where(t, 1, 0) for t in (has_up, has_down, has_left, has_right))
    pl.semaphore_wait(barrier, expected)

    def remote(which, src_ref, dst_ref, device):
        return pltpu.make_async_remote_copy(
            src_ref=src_ref, dst_ref=dst_ref,
            send_sem=send.at[which], recv_sem=recv.at[which],
            device_id=device, device_id_type=MESH,
        )

    tile_rows = pl.ds(RIM, ROWS)
    k_top, k_low = pl.ds(RIM, DEEP + 1), pl.ds(RIM + ROWS - DEEP - 1, DEEP + 1)
    k_above, k_below = pl.ds(RIM - DEEP - 1, DEEP + 1), pl.ds(RIM + ROWS, DEEP + 1)
    above_rows, below_rows = pl.ds(0, RIM), pl.ds(RIM + ROWS, RIM)
    st_top, st_low = pl.ds(RIM, DEEP), pl.ds(RIM + ROWS - DEEP, DEEP)
    st_above, st_below = pl.ds(RIM - DEEP, DEEP), pl.ds(RIM + ROWS, DEEP)
    design_copy = remote(DESIGN, design_ref.at[pl.ds(SLOTS - SENT, SENT)], ext.at[pl.ds(0, SENT)], nxt)
    st_left = remote(ST_L, st.at[:, 0, tile_rows], st_r, left)
    st_right = remote(ST_R, st.at[:, STRIPS - 1, tile_rows], st_l, right)
    st_up = remote(ST_U, st.at[:, :, st_top], st.at[:, :, st_below], up)
    st_down = remote(ST_D, st.at[:, :, st_low], st.at[:, :, st_above], down)
    k_left = remote(K_L, cond.at[0, tile_rows], k_r, left)
    k_right = remote(K_R, cond.at[STRIPS - 1, tile_rows], k_l, right)

    def k_rows(c, strips):
        return (
            remote(K_U + c, cond.at[strips, k_top], cond.at[strips, k_below], up), has_up,
            remote(K_D + c, cond.at[strips, k_low], cond.at[strips, k_above], down), has_down,
        )

    k_corners = k_rows(GROUPS, pl.ds(STRIPS, 1))

    def start_pair(first, has_first, second, has_second):
        pl.when(has_first)(first.start)
        pl.when(has_second)(second.start)

    def wait_pair(first, has_first, second, has_second):
        pl.when(has_first)(first.wait_send)
        pl.when(has_second)(second.wait_send)
        pl.when(has_second)(first.wait_recv)
        pl.when(has_first)(second.wait_recv)

    design_copy.start()

    for load in loads[:3]:
        load.wait()
    for g in range(STRIPS):
        cols = pl.ds(g * 128, 128)
        solid = raw_holes[:, cols] <= 0
        st[0, g, tile_rows, :] = jnp.where(solid, raw[0, :, cols], 0.0)
        st[1, g, tile_rows, :] = jnp.where(solid, raw[1, :, cols], 0.0)
    start_pair(st_left, has_left, st_right, has_right)

    blocks[...] = jnp.zeros(blocks.shape, jnp.float32)
    for k in range(5):
        tile = tiles_ref[k]
        turned = tile.T
        rows = pl.ds(k * 128, 128)
        hi, lo = split(turned)
        wf[rows, pl.ds(0, 128)] = hi
        wf[rows, pl.ds(128, 128)] = lo
        hi, lo = split(tile)
        wb[rows, pl.ds(0, 128)] = hi
        wb[rows, pl.ds(128, 128)] = lo
        sums[pl.ds(k, 1), :] = jnp.sum(turned, axis=0, keepdims=True)

    for there, value in ((has_left, st_l), (has_right, st_r)):
        @pl.when(jnp.logical_not(there))
        def _():
            value[...] = jnp.zeros(value.shape, jnp.float32)
    for there, value in ((has_left, k_l), (has_right, k_r)):
        @pl.when(jnp.logical_not(there))
        def _():
            value[...] = jnp.zeros(value.shape, jnp.float32)
    for there, rows in ((has_up, above_rows), (has_down, below_rows)):
        @pl.when(jnp.logical_not(there))
        def _():
            st[:, :, rows, :] = jnp.zeros((2, WIDE, RIM, 128), jnp.float32)
            cond[:, rows, :] = jnp.zeros((WIDE, RIM, 128), jnp.float32)

    wait_pair(st_left, has_left, st_right, has_right)
    lane = lax.broadcasted_iota(jnp.int32, (ROWS, 128), 1)
    for q in range(2):
        st[q, STRIPS, tile_rows, :] = jnp.where(lane < 64, st_r[q], st_l[q])
    start_pair(st_up, has_up, st_down, has_down)

    first = slot_ref[0]
    block_row, block_col = (first // 128) % 16, first % 128
    stagger = (block_col // 16) * 256
    for level in range(4):
        stagger = stagger + (block_col // 2**level) % 2 * 4**level
        stagger = stagger + (block_row // 2**level) % 2 * (2 * 4**level)

    loads[3].wait()
    design_copy.wait()
    offset = SENT - stagger

    def place(c, _):
        group = ext[pl.ds(offset + c * GROUP, GROUP), :]
        for (row, half), value in curve_to_rows(group).items():
            at = pl.multiple_of(8 + 16 * c + 8 * half, 8)
            blocks[1 + row, pl.ds(at, 8), :] = value
        return 0

    lax.fori_loop(0, GROUPS, place, 0)

    def near(c):
        def take(row, col):
            return blocks[pl.ds(1 + row, 16), pl.ds(8 + 16 * c + col, 16), :].reshape(GROUP, 128)
        return take

    def denominator(c, width, count):
        row = lax.broadcasted_iota(jnp.int32, (16, width, 128), 0)
        col = lax.broadcasted_iota(jnp.int32, (16, width, 128), 1) + c * width
        total = jnp.broadcast_to(sums[pl.ds(0, 1), :].reshape(1, 1, 128), row.shape)
        inside = (row > 0, row < 15, col > 0, col < 127)
        for k in range(4):
            total = total + jnp.where(inside[k], sums[pl.ds(k + 1, 1), :].reshape(1, 1, 128), 0.0)
        return total.reshape(count, 128)

    def forward(c):
        take = near(c)
        lhs = jnp.concatenate([take(0, 0), take(-1, 0), take(1, 0), take(0, -1), take(0, 1)], axis=1)
        filtered = product(lhs, wf[...]) / denominator(c, 16, GROUP)
        for row in range(16):
            for half in range(2):
                at = row * 16 + 8 * half
                film = flip_block(filtered[at : at + 8])
                dens[2 * c + half, pl.ds(row * 8, 8), :] = film
                cond[2 * c + half, pl.ds(RIM + row * 8, 8), :] = (
                    COND_FLOOR + (1.0 - COND_FLOOR) * film * film * film
                )

    def two_forward(index, _):
        pair = [lax.rem((2 * index + i) * (GROUPS - 1), GROUPS) for i in range(2)]
        for c in pair:
            forward(c)
        for c in pair:
            start_pair(*k_rows(c, pl.ds(2 * c, 2)))
        pl.when((index == 0) & has_left)(k_left.start)
        pl.when((index == 0) & has_right)(k_right.start)
        return 0

    lax.fori_loop(0, GROUPS // 2, two_forward, 0)
    wait_pair(k_left, has_left, k_right, has_right)
    cond[STRIPS, tile_rows, :] = jnp.where(lane < 64, k_r[...], k_l[...])
    start_pair(*k_corners)

    lane8 = lax.broadcasted_iota(jnp.int32, (8, 128), 1)

    def sides(row):
        out = []
        for g in range(WIDE):
            west = pltpu.roll(jnp.where(lane8 == 127, row[g - 1], row[g]), 1, 1)
            east = pltpu.roll(jnp.where(lane8 == 0, row[(g + 1) % WIDE], row[g]), 127, 1)
            out.append((west, east))
        return out

    def coefficients(step):
        r = pl.multiple_of(step * 8, 8)
        here = [cond[g, pl.ds(r, 8), :] for g in range(WIDE)]
        beside = sides(here)
        for g in range(WIDE):
            k = here[g]
            north = 0.5 * (k + cond[g, pl.ds(r - 1, 8), :])
            south = 0.5 * (k + cond[g, pl.ds(r + 1, 8), :])
            west = 0.5 * (k + beside[g][0])
            east = 0.5 * (k + beside[g][1])
            inverse = 1.0 / (north + south + west + east + SQUEEZE_DAMPING)
            solid = st[1, g, pl.ds(r, 8), :] > 0.0
            for ref, face in ((wn, north), (ws, south), (ww, west), (we, east)):
                ref[g, pl.ds(r, 8), :] = jnp.where(solid, face * inverse, 0.0)
            for q in range(2):
                value = st[q, g, pl.ds(r, 8), :] * inverse
                src[q, g, pl.ds(r, 8), :] = value
                ping[q, g, pl.ds(r, 8), :] = value

    def both(first, second):
        def run(index, _):
            coefficients(first + index)
            coefficients(second + index)
            return 0
        return run

    lax.fori_loop(0, 7, both(4, 11), 0)
    wait_pair(st_up, has_up, st_down, has_down)

    def rows_arrived(c, _):
        wait_pair(*k_rows(c, pl.ds(2 * c, 2)))
        return 0

    lax.fori_loop(0, GROUPS, rows_arrived, 0)
    wait_pair(*k_corners)
    lax.fori_loop(0, 3, both(1, 18), 0)

    def sweep(old, new, first_step, last_step, unroll):
        def row_of_strips(r):
            rows = pl.ds(r, 8)
            here = {(q, g): old[q, g, rows, :] for q in range(2) for g in (STRIPS, 0)}
            for g in range(WIDE):
                before, after = (g + STRIPS) % WIDE, (g + 1) % WIDE
                faces = [ref[g, rows, :] for ref in (wn, ws, ww, we)]
                for q in range(2):
                    if (q, after) not in here:
                        here[q, after] = old[q, after, rows, :]
                    mine = here[q, g]
                    west = pltpu.roll(jnp.where(lane8 == 127, here[q, before], mine), 1, 1)
                    east = pltpu.roll(jnp.where(lane8 == 0, here[q, after], mine), 127, 1)
                    north = old[q, g, pl.ds(r - 1, 8), :]
                    south = old[q, g, pl.ds(r + 1, 8), :]
                    new[q, g, rows, :] = (
                        src[q, g, rows, :] + faces[0] * north + faces[1] * south
                    ) + (faces[2] * west + faces[3] * east)

        def several(step, _):
            for part in range(unroll):
                row_of_strips(pl.multiple_of((first_step + unroll * step + part) * 8, 8))
            return 0

        lax.fori_loop(0, (last_step - first_step) // unroll, several, 0)

    def two_deep(_, carry):
        sweep(ping, pong, 1, 21, 5)
        sweep(pong, ping, 1, 21, 5)
        return carry

    def two_shallow(_, carry):
        sweep(pong, ping, 2, 20, 6)
        sweep(ping, pong, 2, 20, 6)
        return carry

    lax.fori_loop(0, 3, two_deep, 0)
    sweep(ping, pong, 1, 21, 5)
    lax.fori_loop(0, (SWEEPS - 8) // 2, two_shallow, 0)

    def gradient(g):
        summed = jnp.zeros((ROWS, 128), jnp.float32)
        p = pong[0, g, tile_rows, :]
        a = pong[1, g, tile_rows, :]
        out[:, pl.ds(g * 128 if isinstance(g, int) else pl.multiple_of(g * 128, 128), 128)] = p
        for shift in (RIM - 1, RIM + 1):
            rows = pl.ds(shift, ROWS)
            summed = summed + (a - pong[1, g, rows, :]) * (p - pong[0, g, rows, :])
        west, east = lax.rem(g + STRIPS, WIDE), g + 1
        for edge, strip, turn in ((127, west, 1), (0, east, 127)):
            pn = pltpu.roll(jnp.where(lane == edge, pong[0, strip, tile_rows, :], p), turn, 1)
            an = pltpu.roll(jnp.where(lane == edge, pong[1, strip, tile_rows, :], a), turn, 1)
            summed = summed + (a - an) * (p - pn)
        density = dens[g]
        sens = -0.5 * summed * (3.0 * (1.0 - COND_FLOOR)) * density * density
        scale = denominator(g, 8, ROWS)
        at = 8 + 8 * g if isinstance(g, int) else pl.multiple_of(8 + 8 * g, 8)
        for row in range(16):
            part = slice(row * 8, row * 8 + 8)
            blocks[1 + row, pl.ds(at, 8), :] = flip_block(sens[part]) / scale[part]

    def back_copy(c):
        return remote(BACK + c, curve.at[pl.ds(c * GROUP, GROUP)], curve.at[pl.ds(SLOTS + c * GROUP, GROUP)], prv)

    def backward(c):
        take = near(c)
        lhs = jnp.concatenate([take(0, 0), take(1, 0), take(-1, 0), take(0, 1), take(0, -1)], axis=1)
        for v, value in enumerate(rows_to_curve(product(lhs, wb[...]))):
            at = c * GROUP + 8 * v
            if not isinstance(at, int):
                at = pl.multiple_of(at, 8)
            curve[pl.ds(at, 8), :] = value

    def back(c, _):
        gradient(2 * c + 1)
        gradient(2 * c + 2)
        backward(c)
        back_copy(c).start()
        return 0

    gradient(0)
    lax.fori_loop(0, SENT_GROUPS, back, 0)
    gradient(13)
    gradient(14)
    backward(6)
    gradient(15)
    pressure_copy = pltpu.make_async_copy(out, pressure_ref, here_sem.at[0])
    pressure_copy.start()
    backward(7)

    def give(c):
        at = c * GROUP
        sens_ref[pl.ds(at, GROUP), :] = curve[pl.ds(stagger + at, GROUP), :]

    for c in range(SENT_GROUPS):
        back_copy(c).wait()
    for c in range(GROUPS):
        give(c)
    pressure_copy.wait()


def solution(mesh):
    n_wide, n_narrow = mesh.shape["wide"], mesh.shape["narrow"]
    f32, bf16 = jnp.float32, jnp.bfloat16
    vmem = pl.BlockSpec(memory_space=pltpu.VMEM)
    anywhere = pl.BlockSpec(memory_space=pl.ANY)

    def local(design, filter_tiles, filter_cols, slot_block, holes, squeeze_source, force_weight):
        strips = (WIDE, TALL, 128)
        return pl.pallas_call(
            functools.partial(body, n_wide, n_narrow),
            out_shape=(
                jax.ShapeDtypeStruct(holes.shape, f32),
                jax.ShapeDtypeStruct(design.shape, f32),
            ),
            in_specs=[pl.BlockSpec(memory_space=pltpu.SMEM), anywhere, vmem] + [anywhere] * 3,
            out_specs=(anywhere, vmem),
            scratch_shapes=[
                pltpu.VMEM((SENT + SLOTS + 8, 128), f32),
                pltpu.VMEM((18, 144, 128), f32),
                pltpu.VMEM((SENT + SLOTS + 8, 128), f32),
                pltpu.VMEM((640, 256), bf16),
                pltpu.VMEM((640, 256), bf16),
                pltpu.VMEM((8, 128), f32),
                pltpu.VMEM((2,) + strips, f32),
                pltpu.VMEM((2, ROWS, 128), f32),
                pltpu.VMEM((2, ROWS, 128), f32),
                pltpu.VMEM((ROWS, 128), f32),
                pltpu.VMEM((ROWS, 128), f32),
                pltpu.VMEM(strips, f32),
                pltpu.VMEM((STRIPS, ROWS, 128), f32),
                pltpu.VMEM(strips, f32),
                pltpu.VMEM(strips, f32),
                pltpu.VMEM(strips, f32),
                pltpu.VMEM(strips, f32),
                pltpu.VMEM((2,) + strips, f32),
                pltpu.VMEM((2,) + strips, f32),
                pltpu.VMEM((2,) + strips, f32),
                pltpu.VMEM((2,) + holes.shape, f32),
                pltpu.VMEM(holes.shape, jnp.int32),
                pltpu.VMEM(holes.shape, f32),
                pltpu.SemaphoreType.DMA((COPIES,)),
                pltpu.SemaphoreType.DMA((COPIES,)),
                pltpu.SemaphoreType.DMA((4,)),
            ],
            compiler_params=pltpu.CompilerParams(
                collective_id=0, has_side_effects=True, vmem_limit_bytes=56 * 2**20
            ),
        )(slot_block, design, filter_tiles, holes, squeeze_source, force_weight)

    placed = (
        P(("wide", "narrow"), None),
        P(),
        P(("wide", "narrow"), None),
        P(("wide", "narrow")),
        P("wide", "narrow"),
        P("wide", "narrow"),
        P("wide", "narrow"),
    )
    return jax.shard_map(
        local,
        mesh=mesh,
        in_specs=placed,
        out_specs=(P("wide", "narrow"), P(("wide", "narrow"), None)),
        check_vma=False,
    )
```
